32 devices in a mesh: sub: 4 (over z), rng: 8 (over y, x, core).
Axes of the slice: x: 2, y: 2, z: 4, core: 2. Of those that a mesh axis runs over, the one named last changes fastest.
Arguments:
- echoes: bfloat16 [2, 2048, 4096], P(None, 'sub', 'rng'), may hold values from -6 to 6
- chirp: bfloat16 [2, 512], replicated, may hold values from -0.1875 to 0.1875
- offsets: int32 [2, 4, 2, 512], P(None, 'sub'), may hold values from 0 to 504
- weights: bfloat16 [2, 4, 2, 2, 512, 8], P(None, 'sub'), may hold values from -1 to 1
- owners: int32 [4, 8, 512, 1], P('sub', 'rng'), may hold values from 0 to 31; in each aligned block of 512 rows (0 to 511, 512 to 1023, ..., all dimensions but the last counted through in order) at most 32 rows name the same one
- targets: int32 [4, 8, 512], P('sub', 'rng'), may hold values from 0 to 511
Outputs:
- tiles: bfloat16 [2, 2048, 4096], P(None, 'sub', 'rng')
The draws below stay inside these ranges and needn't reach their ends.
Inputs may be any that keep to these rules, and one draw needn't show every extreme that they name: `owners`: within the 512 rows of one device, no tile is named more than 32 times, a bound that some block reaches.
All inputs are finite; a program needn't handle non-finite values.
Results may differ from the reference program's by a relative error of at most 0.0069.
Values may be sent and summed in bfloat16 or wider, within the bound.
A program may use at most 384 MiB of HBM per device.

```python
import math
import jax
import jax.numpy as jnp
import numpy as np
from jax import lax

P_DEV = 512
R_DEV = 512
CHIRP = 512
RBLK = 512
TAPS = 8
SECTIONS = 2
SUBS = 4
BLOCKS = 8
PULSES = 2048
RANGE = 4096
TILE_ROWS = 512
CAP = 32
DEVICES = 32


def touch_ends(drawn, stream_key, smallest, high):
    shape = drawn.shape
    spot = [jax.random.randint(jax.random.fold_in(stream_key, axis), (), 0, shape[axis]) for axis in range(len(shape))]
    drawn = drawn.at[tuple(spot)].set(smallest)
    longest = shape.index(max(shape))
    spot[longest] = (spot[longest] + 1) % shape[longest]
    return drawn.at[tuple(spot)].set(high)


def block_levels(own_key, dims, split, least, largest):
    def one(position, blocks):
        draws = jax.random.uniform(jax.random.fold_in(jax.random.fold_in(own_key, 6), position), (blocks,), jnp.float32, least / len(split), largest / len(split))
        return jnp.repeat(jnp.exp(draws), dims[position] // blocks).reshape((-1,) + (1,) * (len(dims) - position - 1))

    gain = one(*split[0])
    for cut in split[1:]:
        gain = gain * one(*cut)
    return gain


def shared_out(stream_key, own, number, rows, number_of, top, reach, slope):
    order = jax.random.permutation(stream_key, number_of)
    heavy_load, usual = portions_of(number_of, rows * top, reach, slope, True), portions_of(number_of, rows * top, reach, slope, False)
    places = jnp.arange(number_of)

    def named(tallies, offset_by):
        used = int((tallies > 0).sum())
        fixed = max(1, used // 4)
        moved = fixed + (places - fixed + offset_by * (used - fixed)) % max(1, number_of - fixed)
        return jnp.zeros((number_of,), jnp.int32).at[order[jnp.where(places < fixed, places, moved)]].set(jnp.asarray(tallies, jnp.int32))

    tallies = jnp.where(number % 4 == 0, named(heavy_load, number // 4), named(usual, number - number // 4 - 1))
    mixed = jax.random.permutation(jax.random.fold_in(own, 3), number_of)
    source_of, sink = mixed[0:number_of // 2 * 2:2], mixed[1:number_of // 2 * 2:2]
    slack = jnp.minimum(tallies[source_of] - 1, reach - tallies[sink]) // 2
    slack = jnp.where((source_of == order[0]) | (sink == order[0]) | (tallies[sink] == 0), 0, jnp.maximum(slack, 0))
    moved = jax.random.randint(jax.random.fold_in(own, 4), (number_of // 2,), 0, 1 << 20) % (slack + 1)
    tallies = tallies.at[source_of].add(-moved).at[sink].add(moved)
    members = jnp.searchsorted(jnp.cumsum(tallies), jnp.arange(rows * top), side="right").astype(jnp.int32)
    table = members.reshape(top, rows).T
    table = table[jax.random.permutation(jax.random.fold_in(own, 1), rows)]
    offset_by = jax.random.randint(jax.random.fold_in(own, 2), (rows, 1), 0, top)
    return jnp.take_along_axis(table, (jnp.arange(top)[None, :] + offset_by) % top, axis=1)


def portions_of(number_of, total, bound, lean, full):
    weights = [(1 << 20) // math.isqrt(rank ** lean) + 1 for rank in range(1, number_of + 1)]
    largest = bound if full else min(bound, max(-(-total // number_of), total * weights[0] // sum(weights)))
    least = 1 if total - largest >= number_of - 1 else 0
    given, rest = [largest] + [least] * (number_of - 1), total - largest - least * (number_of - 1)
    while rest > 0:
        candidates = [i for i in range(1, number_of) if given[i] < largest] or [i for i in range(1, number_of) if given[i] < bound]
        whole, remaining = sum([weights[i] for i in candidates]), rest
        for i in candidates:
            addition = min(bound - given[i], max(1, remaining * weights[i] // whole), rest)
            given[i] = given[i] + addition
            rest = rest - addition
    return np.array(given)


def scatter_about(key, dims, scale, most, cuts=(), kind=jnp.bfloat16):
    level = block_levels(key, dims, cuts, -0.22, 0.18) if cuts else 1.0
    array = jax.random.normal(key, dims, jnp.float32) * scale * level
    return jnp.minimum(jnp.maximum(array, -most), most).astype(kind)


def setup_inputs(seed: int = 0) -> dict:
    key_list = jax.random.split(jax.random.key(seed), 7)
    echoes = scatter_about(key_list[0], (2, PULSES, RANGE), 1.0, 6.0, ((1, 4), (2, 8)))
    chirp = scatter_about(key_list[1], (2, CHIRP), (2 * CHIRP) ** -0.5, 0.1875)
    offsets = touch_ends(jax.random.randint(key_list[2], (SECTIONS, SUBS, 2, P_DEV), 0, P_DEV - TAPS + 1), jax.random.fold_in(key_list[2], 1), 0, P_DEV - TAPS).astype(jnp.int32)
    weights = scatter_about(key_list[3], (SECTIONS, SUBS, 2, 2, P_DEV, TAPS), (4 * TAPS) ** -0.5, 1.0, ((1, 4),))
    owners_keys = jax.random.split(jax.random.fold_in(key_list[4], 1), SUBS * BLOCKS * P_DEV // P_DEV)
    owners_turns = jax.random.permutation(jax.random.fold_in(key_list[4], 3), SUBS * BLOCKS * P_DEV // P_DEV)
    owners = jax.vmap(lambda own, number: shared_out(jax.random.fold_in(key_list[4], 2), own, number, P_DEV, DEVICES, 1, CAP, 2))(owners_keys, owners_turns).reshape((SUBS, BLOCKS, P_DEV, 1))
    targets = touch_ends(jax.random.randint(key_list[5], (SUBS, BLOCKS, P_DEV), 0, TILE_ROWS), jax.random.fold_in(key_list[5], 1), 0, TILE_ROWS - 1).astype(jnp.int32)
    return {"echoes": echoes, "chirp": chirp, "offsets": offsets, "weights": weights, "owners": owners, "targets": targets}


def replica_matrix(chirp, block_len):
    taps_len = chirp.shape[1]
    width = block_len + taps_len
    parts = []
    for part in range(2):
        padded = jnp.concatenate([chirp[part], jnp.zeros((width + 1 - taps_len,), chirp.dtype)])
        tiled = jnp.tile(padded, block_len)[: block_len * width].reshape(block_len, width)
        parts.append(tiled.T)
    h_real, h_imag = parts[0], parts[1]
    upper = jnp.concatenate([h_real, -h_imag], axis=1)
    lower = jnp.concatenate([h_imag, h_real], axis=1)
    return jnp.concatenate([upper, lower], axis=0)


def reference(echoes, chirp, offsets, weights, owners, targets):
    matrix = replica_matrix(chirp, RBLK)
    padded = jnp.pad(echoes, ((0, 0), (0, 0), (0, CHIRP)))

    def compress(index):
        window = lax.dynamic_slice_in_dim(padded, index * RBLK, RBLK + CHIRP, 2)
        stacked = jnp.concatenate([window[0], window[1]], axis=1)
        return jnp.dot(stacked, matrix, preferred_element_type=jnp.float32).astype(jnp.bfloat16)

    count_blocks = RANGE // RBLK
    pieces = lax.map(compress, jnp.arange(count_blocks, dtype=jnp.int32))
    compressed = pieces.reshape(count_blocks, PULSES, 2, RBLK).transpose(2, 1, 0, 3).reshape(2, PULSES, RANGE)
    image = compressed.reshape(2, SUBS, P_DEV, RANGE).transpose(1, 0, 2, 3)
    for section in range(SECTIONS):
        order = np.arange(SUBS) ^ (1 << section)
        sources = (image, image[order])
        real_acc = jnp.zeros((SUBS, P_DEV, RANGE), jnp.float32)
        imag_acc = jnp.zeros((SUBS, P_DEV, RANGE), jnp.float32)
        for side in range(2):
            for tap in range(TAPS):
                index = (offsets[section, :, side, :] + tap).astype(jnp.int32)
                taken = jnp.take_along_axis(sources[side], index[:, None, :, None], axis=2).astype(jnp.float32)
                w_real = weights[section, :, side, 0, :, tap].astype(jnp.float32)[:, :, None]
                w_imag = weights[section, :, side, 1, :, tap].astype(jnp.float32)[:, :, None]
                real_acc = real_acc + w_real * taken[:, 0] - w_imag * taken[:, 1]
                imag_acc = imag_acc + w_real * taken[:, 1] + w_imag * taken[:, 0]
        image = jnp.stack([real_acc, imag_acc], axis=1).astype(jnp.bfloat16)
    rows = image.reshape(SUBS, 2, P_DEV, BLOCKS, R_DEV).transpose(0, 3, 2, 1, 4).reshape(SUBS * BLOCKS * P_DEV, 2, R_DEV)
    flat_index = (owners.reshape(-1) * TILE_ROWS + targets.reshape(-1)).astype(jnp.int32)
    summed = jnp.zeros((DEVICES * TILE_ROWS, 2, R_DEV), jnp.float32).at[flat_index].add(rows.astype(jnp.float32))
    result = summed.reshape(SUBS, BLOCKS, TILE_ROWS, 2, R_DEV).transpose(3, 0, 2, 1, 4)
    return result.reshape(2, SUBS * TILE_ROWS, RANGE).astype(jnp.bfloat16)
```

```python
import functools

import jax
import jax.numpy as jnp
from jax import lax
from jax.experimental import pallas as pl
from jax.experimental.pallas import tpu as pltpu
from jax.sharding import PartitionSpec as P

MESH = pl.DeviceIdType.MESH
BF = jnp.bfloat16
F32 = jnp.float32
CS = 64
CH = 128
NT = (((1,), (1,)), ((), ()))


def nt(a, b):
    return lax.dot_general(a, b, NT, preferred_element_type=F32)


def nn(a, b):
    return jnp.dot(a, b, preferred_element_type=F32)


def z_of(i, n_sub):
    return (i % 2) * (n_sub // 2) + i // 2


def kernel(
    n_sub, n_rng, sections, stages, cap,
    e_ref, chirp_ref, meta_ref, w_ref, out_ref,
    h_ref, tail, metas, wall, cmp, img, gt, ya, yb, pick, upper, labsend, lab, lrow, place, sbuf, got, tbuf,
    tail_s, tail_r, meta_s, meta_r, w_s, w_r, img_s, img_r, lab_s, lab_r, x_s, x_r, t_s, t_r, loc,
):
    z = lax.axis_index("sub")
    r = lax.axis_index("rng")
    p = e_ref.shape[1]
    rd_len = e_ref.shape[2]
    taps_len = rd_len
    chunks = rd_len // CH
    width = CH + taps_len
    keep = stages > 1
    dests = n_sub * n_rng

    barrier = pltpu.get_barrier_semaphore()
    for d in range(1, n_sub):
        pl.semaphore_signal(barrier, inc=1, device_id=(lax.rem(z + d, n_sub), r), device_id_type=MESH)
    for d in range(1, n_rng):
        pl.semaphore_signal(barrier, inc=1, device_id=(z, lax.rem(r + d, n_rng)), device_id_type=MESH)
    pl.semaphore_wait(barrier, n_sub + n_rng - 2)

    def remote(src, dst, ss, rs, dev):
        return pltpu.make_async_remote_copy(
            src_ref=src, dst_ref=dst, send_sem=ss, recv_sem=rs, device_id=dev, device_id_type=MESH
        )

    def tail_copy(k):
        span = pl.ds(k * CH, CH)
        left = jnp.where(r == 0, 1, r - 1)
        return remote(e_ref.at[:, :, span], tail.at[:, :, span], tail_s.at[k], tail_r.at[k], (z, left))

    @pl.when(r > 0)
    def _():
        for k in range(chunks):
            tail_copy(k).start()

    def meta_copy(src, d):
        peer = lax.rem(z + d, n_sub)
        return (
            remote(meta_ref, metas.at[src], meta_s.at[d], meta_r.at[src], (peer, r)),
            remote(w_ref, wall.at[src], w_s.at[d], w_r.at[src], (peer, r)),
        )

    for d in range(1, n_sub):
        for c in meta_copy(z, d):
            c.start()
    metas[z] = meta_ref[...]
    wall[z] = w_ref[...]

    @pl.when(r == n_rng - 1)
    def _():
        tail[...] = jnp.zeros_like(tail)

    parts = []
    for part in range(2):
        row = jnp.broadcast_to(chirp_ref[pl.ds(part, 1), :], (CH, width))
        parts.append(pltpu.roll(row, 0, 1, stride=1, stride_axis=0))
    h_re, h_im = parts
    h_ref[0, :CH] = h_re.astype(BF)
    h_ref[0, CH:] = (-h_im).astype(BF)
    h_ref[1, :CH] = h_im.astype(BF)
    h_ref[1, CH:] = h_re.astype(BF)

    def build_merge(section, g, slot):
        for side in range(2):
            j = section * 2 + side
            off = metas[g, pl.ds(j, 1), :]
            w = wall[g, j].astype(F32)
            spot = lax.broadcasted_iota(jnp.int32, (p, p), 0) - off
            hit = (spot >= 0) & (spot < 8)
            for part in range(2):
                wide = jnp.broadcast_to(w[part * 8 : part * 8 + 8][None], (p // 8, 8, p)).reshape(p, p)
                gt[slot, side, part] = jnp.where(hit, wide, 0.0).astype(BF)

    def build_pick(g, slot):
        owner = metas[g, pl.ds(6, 1), :]
        aim = metas[g, pl.ds(7, 1), :]
        onehot = jnp.where(lax.broadcasted_iota(jnp.int32, (dests, p), 0) == owner, 1.0, 0.0)
        before = nn(onehot.astype(BF), upper[...])
        rank = jnp.sum(onehot * before, axis=0, keepdims=True).astype(jnp.int32)
        zd = owner // n_rng
        where_to = ((owner - zd * n_rng) * n_sub + zd) * cap + rank
        hit = lax.broadcasted_iota(jnp.int32, (dests * cap, p), 0) == where_to
        pick[slot] = jnp.where(hit, 1.0, 0.0).astype(BF)
        mark = aim + 1
        hi = mark // 16
        lo = mark - hi * 16
        rows = lax.broadcasted_iota(jnp.int32, (16, p), 0)
        both = jnp.where(rows == 0, hi, jnp.where(rows == 1, lo, 0)).astype(F32).astype(BF)
        out = nt(both, pick[slot])
        label = out[0:1] * 16.0 + out[1:2] - 1.0
        for rd in range(n_rng):
            labsend[rd, pl.ds(g, 1), :] = label[:, rd * 128 : (rd + 1) * 128]

    before = lax.broadcasted_iota(jnp.int32, (p, p), 0) < lax.broadcasted_iota(jnp.int32, (p, p), 1)
    upper[...] = jnp.where(before, 1.0, 0.0).astype(BF)

    def img_copy(s, i, src):
        sub = s * n_sub + i
        k, o = sub // (CH // CS), sub % (CH // CS)
        view = cmp.at[k, :, pl.ds(o * CS, CS), :]
        zd = z_of(i, n_sub)
        return view, remote(view, img.at[s, src], img_s.at[s, i], img_r.at[s, src], (zd, r))

    def wait_meta(g):
        @pl.when(z != g)
        def _():
            for c in meta_copy(g, 1):
                c.wait_recv()

    for k in range(chunks):
        @pl.when(r < n_rng - 1)
        def _():
            tail_copy(k).wait_recv()

        cut = rd_len - CH * k
        acc = None
        for part in range(2):
            x = nt(h_ref[part, :, :cut], e_ref[part, :, CH * k :])
            y = nt(h_ref[part, :, cut:], tail[part, :, : CH * (k + 1)])
            acc = x + y if acc is None else acc + x + y
        cmp[k] = acc.astype(BF).reshape(2, CH, p)
        for o in range(CH // CS):
            sub = k * (CH // CS) + o
            s, i = sub // n_sub, sub % n_sub
            view, copy = img_copy(s, i, z)
            own = z == z_of(i, n_sub)

            @pl.when(own)
            def _():
                pltpu.make_async_copy(view, img.at[s, z], loc.at[s]).start()

            @pl.when(jnp.logical_not(own))
            def _():
                copy.start()

        if keep and k < n_sub:
            wait_meta(k)
            for section in range(sections):
                build_merge(section, k, section * n_sub + k)
            build_pick(k, k)

    for g in range(chunks if keep else 0, n_sub):
        wait_meta(g)
        if keep:
            for section in range(sections):
                build_merge(section, g, section * n_sub + g)
            build_pick(g, g)

    def lab_copy(src, d):
        peer = lax.rem(r + d, n_rng)
        return remote(labsend.at[peer], lab.at[src], lab_s.at[d], lab_r.at[src], (z, peer))

    def send_labels():
        for d in range(1, n_rng):
            lab_copy(r, d).start()
        lab[r] = labsend[r]

    def x_copy(s, src, d):
        peer = lax.rem(r + d, n_rng)
        return remote(sbuf.at[s, peer], got.at[s, :, src], x_s.at[s, d], x_r.at[s, src], (z, peer))

    def x_local(s):
        return pltpu.make_async_copy(sbuf.at[s, r], got.at[s, :, r], loc.at[stages + s])

    if keep:
        send_labels()

    for s in range(stages):
        pltpu.make_async_copy(img.at[s, z], img.at[s, z], loc.at[s]).wait()
        for d in range(1, n_sub):
            img_copy(s, 0, lax.rem(z + d, n_sub))[1].wait_recv()
        for section in range(sections):
            bit = 1 << section
            dst = (ya, yb)[section % 2]

            def load(g):
                if section == 0:
                    return img[s, g].reshape(2 * CS, p)
                return (ya, yb)[(section + 1) % 2][g]

            def merge(g, carry):
                q = g + bit - 2 * bit * ((g // bit) % 2)
                slot = section * n_sub + g
                if not keep:
                    slot = 0
                    build_merge(section, g, 0)
                own, other = load(g), load(q)
                a = nn(own, gt[slot, 0, 0]) + nn(other, gt[slot, 1, 0])
                b = nn(own, gt[slot, 0, 1]) + nn(other, gt[slot, 1, 1])
                dst[g, :CS] = (a[:CS] - b[CS:]).astype(BF)
                dst[g, CS:] = (a[CS:] + b[:CS]).astype(BF)
                return carry

            lax.fori_loop(0, n_sub, merge, 0)
        final = (ya, yb)[(sections - 1) % 2]

        def gather(g, carry):
            slot = g
            if not keep:
                slot = 0
                build_pick(g, 0)
            rows = nt(pick[slot], final[g]).astype(BF)
            sbuf[s, :, :, pl.ds(pl.multiple_of(g * cap, cap), cap), :] = rows.reshape(n_rng, n_sub, cap, 2 * CS)
            return carry

        lax.fori_loop(0, n_sub, gather, 0)
        for d in range(1, n_rng):
            x_copy(s, r, d).start()
        x_local(s).start()
        if not keep:
            send_labels()

    for d in range(1, n_rng):
        lab_copy(lax.rem(r + d, n_rng), d).wait_recv()
    lane = lax.broadcasted_iota(jnp.int32, (n_rng, 128), 1) // cap
    for zd in range(n_sub):
        total = jnp.zeros((n_rng, 128), F32)
        for g in range(n_sub):
            piece = lab[:, g, :]
            move = ((g - zd) * cap) % 128
            if move:
                piece = pltpu.roll(piece, move, 1)
            total = jnp.where(lane == g, piece, total)
        lrow[zd] = total

    def build_place(zd, slot):
        rows = lax.broadcasted_iota(jnp.int32, (p, 128), 0)
        for j in range(n_rng):
            label = lrow[zd, pl.ds(j, 1), :].astype(jnp.int32)
            place[slot, :, j * 128 : (j + 1) * 128] = jnp.where(rows == label, 1.0, 0.0).astype(BF)

    if keep:
        def run(zd, carry):
            build_place(zd, zd)
            return carry

        lax.fori_loop(0, n_sub, run, 0)

    def t_copy(s, src, zd, d):
        return remote(tbuf.at[s, zd], out_ref.at[s, src], t_s.at[s, d], t_r.at[s, src], (zd, r))

    for s in range(stages):
        x_local(s).wait()
        for d in range(1, n_rng):
            x_copy(s, lax.rem(r + d, n_rng), d).wait_recv()
        for d in list(range(1, n_sub)) + [0]:
            zd = lax.rem(z + d, n_sub)
            slot = zd
            if not keep:
                slot = 0
                build_place(zd, 0)
            tile = nn(place[slot], got[s, zd].reshape(n_rng * 128, 2 * CS)).astype(BF)
            if d:
                tbuf[s, zd] = tile
                t_copy(s, z, zd, d).start()
            else:
                out_ref[s, z] = tile

    for s in range(stages):
        for d in range(1, n_sub):
            peer = lax.rem(z + d, n_sub)
            t_copy(s, peer, peer, d).wait_recv()

    @pl.when(r > 0)
    def _():
        for k in range(chunks):
            tail_copy(k).wait_send()

    for d in range(1, n_sub):
        for c in meta_copy(z, d):
            c.wait_send()
    for s in range(stages):
        for i in range(n_sub):
            @pl.when(z != z_of(i, n_sub))
            def _():
                img_copy(s, i, z)[1].wait_send()

        for d in range(1, n_rng):
            x_copy(s, r, d).wait_send()
        for d in range(1, n_sub):
            t_copy(s, z, lax.rem(z + d, n_sub), d).wait_send()
    for d in range(1, n_rng):
        lab_copy(r, d).wait_send()


def on_device(echoes, chirp, offsets, weights, owners, targets):
    p = echoes.shape[1]
    r_dev = echoes.shape[2]
    n_sub = lax.axis_size("sub")
    n_rng = lax.axis_size("rng")
    devices = n_sub * n_rng
    sections = offsets.shape[0]
    cap = max(16, 2 * p // devices)
    stages = r_dev // (n_sub * CS)
    chunks = r_dev // CH
    keep = stages > 1

    off = offsets[:, 0]
    w = weights[:, 0].transpose(0, 1, 2, 4, 3)
    for bit in (1, 2, 4):
        w = jnp.where((off[:, :, None, None, :] & bit) != 0, jnp.roll(w, bit, axis=3), w)
    w = w.reshape(sections * 2, 16, p)
    meta = jnp.concatenate(
        [
            off.reshape(sections * 2, p),
            jnp.zeros((6 - sections * 2, p), jnp.int32),
            owners.reshape(1, p),
            targets.reshape(1, p),
        ]
    )
    taps = jnp.pad(chirp.astype(F32), ((0, 6), (0, CH)))

    vm = pltpu.VMEM
    dma = pltpu.SemaphoreType.DMA
    built = n_sub if keep else 1
    scratch = [
        vm((2, 2 * CH, CH + r_dev), BF),
        vm((2, p, r_dev), BF),
        vm((n_sub, 8, p), jnp.int32),
        vm((n_sub, sections * 2, 16, p), BF),
        vm((chunks, 2, CH, p), BF),
        vm((stages, n_sub, 2, CS, p), BF),
        vm((built * sections if keep else 1, 2, 2, p, p), BF),
        vm((n_sub, 2 * CS, p), BF),
        vm((n_sub, 2 * CS, p), BF),
        vm((built, devices * cap, p), BF),
        vm((p, p), BF),
        vm((n_rng, 8, 128), F32),
        vm((n_rng, 8, 128), F32),
        vm((n_sub, n_rng, 128), F32),
        vm((built, p, n_rng * 128), BF),
        vm((stages, n_rng, n_sub, n_sub * cap, 2 * CS), BF),
        vm((stages, n_sub, n_rng, n_sub * cap, 2 * CS), BF),
        vm((stages, n_sub, p, 2 * CS), BF),
        dma((chunks,)), dma((chunks,)),
        dma((n_sub,)), dma((n_sub,)),
        dma((n_sub,)), dma((n_sub,)),
        dma((stages, n_sub)), dma((stages, n_sub)),
        dma((n_rng,)), dma((n_rng,)),
        dma((stages, n_rng)), dma((stages, n_rng)),
        dma((stages, n_sub)), dma((stages, n_sub)),
        dma((2 * stages,)),
    ]
    out = pl.pallas_call(
        functools.partial(kernel, n_sub, n_rng, sections, stages, cap),
        out_shape=jax.ShapeDtypeStruct((stages, n_sub, p, 2 * CS), BF),
        in_specs=[pl.BlockSpec(memory_space=pltpu.VMEM)] * 4,
        out_specs=pl.BlockSpec(memory_space=pltpu.VMEM),
        scratch_shapes=scratch,
        compiler_params=pltpu.CompilerParams(
            collective_id=0, has_side_effects=True, vmem_limit_bytes=56 * 1024 * 1024
        ),
        cost_estimate=pl.CostEstimate(flops=8 * 10**9, bytes_accessed=4 * 10**6, transcendentals=0),
    )(echoes, taps, meta, w)
    half = n_sub // 2
    out = out.reshape(stages, 2, half, p, 2, CS).transpose(4, 3, 0, 2, 1, 5)
    return out.reshape(2, p, r_dev)


def solution(mesh):
    in_specs = (
        P(None, "sub", "rng"),
        P(),
        P(None, "sub", None, None),
        P(None, "sub", None, None, None, None),
        P("sub", "rng", None, None),
        P("sub", "rng", None),
    )
    out_specs = P(None, "sub", "rng")
    return jax.shard_map(
        on_device, mesh=mesh, in_specs=in_specs, out_specs=out_specs, check_vma=False
    )
```

```python
import functools

import jax
import jax.numpy as jnp
from jax import lax
from jax.experimental import pallas as pl
from jax.experimental.pallas import tpu as pltpu
from jax.sharding import PartitionSpec as P

MESH = pl.DeviceIdType.MESH
BF = jnp.bfloat16
F32 = jnp.float32
CS = 64
CH = 128
NT = (((1,), (1,)), ((), ()))


def nt(a, b):
    return lax.dot_general(a, b, NT, preferred_element_type=F32)


def nn(a, b):
    return jnp.dot(a, b, preferred_element_type=F32)


def z_of(i, n_sub):
    return (i % 2) * (n_sub // 2) + i // 2


def kernel(
    n_sub, n_rng, sections, stages, cap,
    e_ref, chirp_ref, off_ref, own_ref, aim_ref, w_ref, out_ref,
    h_ref, tail, metas, wall, cmp, img, gt, ya, yb, pick, upper, labsend, lab, lrow, place, sbuf, got, tbuf, obuf,
    tail_s, tail_r, meta_s, meta_r, w_s, w_r, img_s, img_r, lab_s, lab_r, x_s, x_r, t_s, t_r, loc,
):
    z = lax.axis_index("sub")
    r = lax.axis_index("rng")
    p = e_ref.shape[1]
    rd_len = e_ref.shape[2]
    taps_len = rd_len
    chunks = rd_len // CH
    width = CH + taps_len
    keep = stages > 1
    dests = n_sub * n_rng

    barrier = pltpu.get_barrier_semaphore()
    for d in range(1, n_sub):
        pl.semaphore_signal(barrier, inc=1, device_id=(lax.rem(z + d, n_sub), r), device_id_type=MESH)
    for d in range(1, n_rng):
        pl.semaphore_signal(barrier, inc=1, device_id=(z, lax.rem(r + d, n_rng)), device_id_type=MESH)

    taps = chirp_ref[...].astype(F32)
    parts = []
    for part in range(2):
        row = jnp.concatenate([taps[part : part + 1], jnp.zeros((1, CH), F32)], axis=1)
        parts.append(pltpu.roll(jnp.broadcast_to(row, (CH, width)), 0, 1, stride=1, stride_axis=0))
    h_re, h_im = parts
    h_ref[0, :CH] = h_re.astype(BF)
    h_ref[0, CH:] = (-h_im).astype(BF)
    h_ref[1, :CH] = h_im.astype(BF)
    h_ref[1, CH:] = h_re.astype(BF)

    for section in range(sections):
        for side in range(2):
            j = section * 2 + side
            off = off_ref[section, pl.ds(side, 1), :]
            both = []
            for part in range(2):
                w = w_ref[j * 2 + part].astype(F32)
                for bit in (1, 2, 4):
                    odd = jnp.broadcast_to((off // bit) % 2, (8, p)) == 1
                    w = jnp.where(odd, pltpu.roll(w, bit, 0), w)
                both.append(w)
            wall[z, j] = jnp.concatenate(both, axis=0).astype(BF)
            metas[z, pl.ds(j, 1), :] = off
    metas[z, pl.ds(6, 1), :] = own_ref[...]
    metas[z, pl.ds(7, 1), :] = aim_ref[...]
    for j in range(sections * 2, 6):
        metas[z, pl.ds(j, 1), :] = jnp.zeros((1, p), jnp.int32)
    pl.semaphore_wait(barrier, n_sub + n_rng - 2)

    def remote(src, dst, ss, rs, dev):
        return pltpu.make_async_remote_copy(
            src_ref=src, dst_ref=dst, send_sem=ss, recv_sem=rs, device_id=dev, device_id_type=MESH
        )

    def tail_copy(k):
        span = pl.ds(k * CH, CH)
        left = jnp.where(r == 0, 1, r - 1)
        return remote(e_ref.at[:, :, span], tail.at[:, :, span], tail_s.at[k], tail_r.at[k], (z, left))

    @pl.when(r > 0)
    def _():
        for k in range(chunks):
            tail_copy(k).start()

    def meta_copy(src, d):
        peer = lax.rem(z + d, n_sub)
        return (
            remote(metas.at[z], metas.at[src], meta_s.at[d], meta_r.at[src], (peer, r)),
            remote(wall.at[z], wall.at[src], w_s.at[d], w_r.at[src], (peer, r)),
        )

    for d in range(1, n_sub):
        for c in meta_copy(z, d):
            c.start()

    @pl.when(r == n_rng - 1)
    def _():
        tail[...] = jnp.zeros_like(tail)

    def build_merge(section, g, slot):
        for side in range(2):
            j = section * 2 + side
            off = metas[g, pl.ds(j, 1), :]
            w = wall[g, j].astype(F32)
            spot = lax.broadcasted_iota(jnp.int32, (p, p), 0) - off
            hit = (spot >= 0) & (spot < 8)
            for part in range(2):
                wide = jnp.broadcast_to(w[part * 8 : part * 8 + 8][None], (p // 8, 8, p)).reshape(p, p)
                gt[slot, side, part] = jnp.where(hit, wide, 0.0).astype(BF)

    def build_pick(g, slot):
        owner = metas[g, pl.ds(6, 1), :]
        aim = metas[g, pl.ds(7, 1), :]
        onehot = jnp.where(lax.broadcasted_iota(jnp.int32, (dests, p), 0) == owner, 1.0, 0.0)
        before = nn(onehot.astype(BF), upper[...])
        rank = jnp.sum(onehot * before, axis=0, keepdims=True).astype(jnp.int32)
        zd = owner // n_rng
        where_to = ((owner - zd * n_rng) * n_sub + zd) * cap + rank
        hit = lax.broadcasted_iota(jnp.int32, (dests * cap, p), 0) == where_to
        pick[slot] = jnp.where(hit, 1.0, 0.0).astype(BF)
        mark = aim + 1
        hi = mark // 16
        lo = mark - hi * 16
        rows = lax.broadcasted_iota(jnp.int32, (16, p), 0)
        both = jnp.where(rows == 0, hi, jnp.where(rows == 1, lo, 0)).astype(F32).astype(BF)
        out = nt(both, pick[slot])
        label = out[0:1] * 16.0 + out[1:2] - 1.0
        for rd in range(n_rng):
            labsend[rd, pl.ds(g, 1), :] = label[:, rd * 128 : (rd + 1) * 128]

    before = lax.broadcasted_iota(jnp.int32, (p, p), 0) < lax.broadcasted_iota(jnp.int32, (p, p), 1)
    upper[...] = jnp.where(before, 1.0, 0.0).astype(BF)

    def img_copy(s, i, src):
        sub = s * n_sub + i
        k, o = sub // (CH // CS), sub % (CH // CS)
        view = cmp.at[k, :, pl.ds(o * CS, CS), :]
        zd = z_of(i, n_sub)
        return view, remote(view, img.at[s, src], img_s.at[s, i], img_r.at[s, src], (zd, r))

    def wait_meta(g):
        @pl.when(z != g)
        def _():
            for c in meta_copy(g, 1):
                c.wait_recv()

    for k in range(chunks):
        @pl.when(r < n_rng - 1)
        def _():
            tail_copy(k).wait_recv()

        cut = rd_len - CH * k
        acc = None
        for part in range(2):
            x = nt(h_ref[part, :, :cut], e_ref[part, :, CH * k :])
            y = nt(h_ref[part, :, cut:], tail[part, :, : CH * (k + 1)])
            acc = x + y if acc is None else acc + x + y
        cmp[k] = acc.astype(BF).reshape(2, CH, p)
        for o in range(CH // CS):
            sub = k * (CH // CS) + o
            s, i = sub // n_sub, sub % n_sub
            view, copy = img_copy(s, i, z)
            own = z == z_of(i, n_sub)

            @pl.when(own)
            def _():
                pltpu.make_async_copy(view, img.at[s, z], loc.at[s]).start()

            @pl.when(jnp.logical_not(own))
            def _():
                copy.start()

        if keep and k < n_sub:
            wait_meta(k)
            for section in range(sections):
                build_merge(section, k, section * n_sub + k)
            build_pick(k, k)

    for g in range(chunks if keep else 0, n_sub):
        wait_meta(g)
        if keep:
            for section in range(sections):
                build_merge(section, g, section * n_sub + g)
            build_pick(g, g)

    def lab_copy(src, d):
        peer = lax.rem(r + d, n_rng)
        return remote(labsend.at[peer], lab.at[src], lab_s.at[d], lab_r.at[src], (z, peer))

    def send_labels():
        for d in range(1, n_rng):
            lab_copy(r, d).start()
        lab[r] = labsend[r]

    def x_copy(s, src, d):
        peer = lax.rem(r + d, n_rng)
        return remote(sbuf.at[s, peer], got.at[s, :, src], x_s.at[s, d], x_r.at[s, src], (z, peer))

    def x_local(s):
        return pltpu.make_async_copy(sbuf.at[s, r], got.at[s, :, r], loc.at[stages + s])

    if keep:
        send_labels()

    for s in range(stages):
        pltpu.make_async_copy(img.at[s, z], img.at[s, z], loc.at[s]).wait()
        for section in range(sections):
            bit = 1 << section
            dst = (ya, yb)[section % 2]

            def load(g):
                if section == 0:
                    return img[s, g].reshape(2 * CS, p)
                return (ya, yb)[(section + 1) % 2][g]

            def merge(g, carry):
                q = g + bit - 2 * bit * ((g // bit) % 2)
                slot = section * n_sub + g
                if not keep:
                    slot = 0
                    build_merge(section, g, 0)
                own, other = load(g), load(q)
                a = nn(own, gt[slot, 0, 0]) + nn(other, gt[slot, 1, 0])
                b = nn(own, gt[slot, 0, 1]) + nn(other, gt[slot, 1, 1])
                dst[g, :CS] = (a[:CS] - b[CS:]).astype(BF)
                dst[g, CS:] = (a[CS:] + b[:CS]).astype(BF)
                return carry

            if section == 0:
                for away in range(n_sub // 2):
                    pair = lax.rem(z // 2 + away, n_sub // 2)
                    if away == 0:
                        img_copy(s, 0, z + 1 - 2 * (z % 2))[1].wait_recv()
                    else:
                        img_copy(s, 0, 2 * pair)[1].wait_recv()
                        img_copy(s, 0, 2 * pair + 1)[1].wait_recv()
                    lax.fori_loop(2 * pair, 2 * pair + 2, merge, 0)
            else:
                lax.fori_loop(0, n_sub, merge, 0)
        final = (ya, yb)[(sections - 1) % 2]

        def gather(g, carry):
            slot = g
            if not keep:
                slot = 0
                build_pick(g, 0)
            rows = nt(pick[slot], final[g]).astype(BF)
            sbuf[s, :, :, pl.ds(pl.multiple_of(g * cap, cap), cap), :] = rows.reshape(n_rng, n_sub, cap, 2 * CS)
            return carry

        lax.fori_loop(0, n_sub, gather, 0)
        for d in range(1, n_rng):
            x_copy(s, r, d).start()
        x_local(s).start()
        if not keep:
            send_labels()

    for d in range(1, n_rng):
        lab_copy(lax.rem(r + d, n_rng), d).wait_recv()
    lane = lax.broadcasted_iota(jnp.int32, (n_rng, 128), 1) // cap
    for zd in range(n_sub):
        total = jnp.zeros((n_rng, 128), F32)
        for g in range(n_sub):
            piece = lab[:, g, :]
            move = ((g - zd) * cap) % 128
            if move:
                piece = pltpu.roll(piece, move, 1)
            total = jnp.where(lane == g, piece, total)
        lrow[zd] = total

    def build_place(zd, slot):
        rows = lax.broadcasted_iota(jnp.int32, (p, 128), 0)
        for j in range(n_rng):
            label = lrow[zd, pl.ds(j, 1), :].astype(jnp.int32)
            place[slot, :, j * 128 : (j + 1) * 128] = jnp.where(rows == label, 1.0, 0.0).astype(BF)

    if keep:
        def run(zd, carry):
            build_place(zd, zd)
            return carry

        lax.fori_loop(0, n_sub, run, 0)

    def t_copy(s, src, zd, d):
        return remote(tbuf.at[s, zd], obuf.at[s, src], t_s.at[s, d], t_r.at[s, src], (zd, r))

    for s in range(stages):
        x_local(s).wait()
        for d in range(1, n_rng):
            x_copy(s, lax.rem(r + d, n_rng), d).wait_recv()
        for d in list(range(1, n_sub)) + [0]:
            zd = lax.rem(z + d, n_sub)
            slot = zd
            if not keep:
                slot = 0
                build_place(zd, 0)
            tile = nn(place[slot], got[s, zd].reshape(n_rng * 128, 2 * CS)).astype(BF)
            if d:
                tbuf[s, zd] = tile
                t_copy(s, z, zd, d).start()
            else:
                obuf[s, z] = tile

    for s in range(stages):
        for d in range(1, n_sub):
            peer = lax.rem(z + d, n_sub)
            t_copy(s, peer, peer, d).wait_recv()
        for i in range(0, n_sub, 2):
            low, high = obuf[s, z_of(i, n_sub)], obuf[s, z_of(i + 1, n_sub)]
            span = slice((s * n_sub + i) * CS, (s * n_sub + i + 2) * CS)
            out_ref[0, :, span] = jnp.concatenate([low[:, :CS], high[:, :CS]], axis=1)
            out_ref[1, :, span] = jnp.concatenate([low[:, CS:], high[:, CS:]], axis=1)

    @pl.when(r > 0)
    def _():
        for k in range(chunks):
            tail_copy(k).wait_send()

    for d in range(1, n_sub):
        for c in meta_copy(z, d):
            c.wait_send()
    for s in range(stages):
        for i in range(n_sub):
            @pl.when(z != z_of(i, n_sub))
            def _():
                img_copy(s, i, z)[1].wait_send()

        for d in range(1, n_rng):
            x_copy(s, r, d).wait_send()
        for d in range(1, n_sub):
            t_copy(s, z, lax.rem(z + d, n_sub), d).wait_send()
    for d in range(1, n_rng):
        lab_copy(r, d).wait_send()


def on_device(echoes, chirp, offsets, weights, owners, targets):
    p = echoes.shape[1]
    r_dev = echoes.shape[2]
    n_sub = lax.axis_size("sub")
    n_rng = lax.axis_size("rng")
    devices = n_sub * n_rng
    sections = offsets.shape[0]
    cap = max(16, 2 * p // devices)
    stages = r_dev // (n_sub * CS)
    chunks = r_dev // CH
    keep = stages > 1
    vm = pltpu.VMEM
    dma = pltpu.SemaphoreType.DMA
    built = n_sub if keep else 1
    scratch = [
        vm((2, 2 * CH, CH + r_dev), BF),
        vm((2, p, r_dev), BF),
        vm((n_sub, 8, p), jnp.int32),
        vm((n_sub, sections * 2, 16, p), BF),
        vm((chunks, 2, CH, p), BF),
        vm((stages, n_sub, 2, CS, p), BF),
        vm((built * sections if keep else 1, 2, 2, p, p), BF),
        vm((n_sub, 2 * CS, p), BF),
        vm((n_sub, 2 * CS, p), BF),
        vm((built, devices * cap, p), BF),
        vm((p, p), BF),
        vm((n_rng, 8, 128), F32),
        vm((n_rng, 8, 128), F32),
        vm((n_sub, n_rng, 128), F32),
        vm((built, p, n_rng * 128), BF),
        vm((stages, n_rng, n_sub, n_sub * cap, 2 * CS), BF),
        vm((stages, n_sub, n_rng, n_sub * cap, 2 * CS), BF),
        vm((stages, n_sub, p, 2 * CS), BF),
        vm((stages, n_sub, p, 2 * CS), BF),
        dma((chunks,)), dma((chunks,)),
        dma((n_sub,)), dma((n_sub,)),
        dma((n_sub,)), dma((n_sub,)),
        dma((stages, n_sub)), dma((stages, n_sub)),
        dma((n_rng,)), dma((n_rng,)),
        dma((stages, n_rng)), dma((stages, n_rng)),
        dma((stages, n_sub)), dma((stages, n_sub)),
        dma((2 * stages,)),
    ]
    return pl.pallas_call(
        functools.partial(kernel, n_sub, n_rng, sections, stages, cap),
        out_shape=jax.ShapeDtypeStruct((2, p, r_dev), BF),
        in_specs=[pl.BlockSpec(memory_space=pltpu.VMEM)] * 6,
        out_specs=pl.BlockSpec(memory_space=pltpu.VMEM),
        scratch_shapes=scratch,
        compiler_params=pltpu.CompilerParams(
            collective_id=0, has_side_effects=True, vmem_limit_bytes=56 * 1024 * 1024
        ),
        cost_estimate=pl.CostEstimate(flops=8 * 10**9, bytes_accessed=4 * 10**6, transcendentals=0),
    )(
        echoes,
        chirp,
        offsets[:, 0],
        owners.reshape(1, p),
        targets.reshape(1, p),
        weights.transpose(0, 1, 2, 3, 5, 4).reshape(sections * 4, weights.shape[-1], p),
    )


def solution(mesh):
    in_specs = (
        P(None, "sub", "rng"),
        P(),
        P(None, "sub", None, None),
        P(None, "sub", None, None, None, None),
        P("sub", "rng", None, None),
        P("sub", "rng", None),
    )
    out_specs = P(None, "sub", "rng")
    return jax.shard_map(
        on_device, mesh=mesh, in_specs=in_specs, out_specs=out_specs, check_vma=False
    )
```

```python
import functools

import jax
import jax.numpy as jnp
from jax import lax
from jax.experimental import pallas as pl
from jax.experimental.pallas import tpu as pltpu
from jax.sharding import PartitionSpec as P

MESH = pl.DeviceIdType.MESH
BF = jnp.bfloat16
F32 = jnp.float32
CS = 64
CH = 128
NT = (((1,), (1,)), ((), ()))


def nt(a, b):
    return lax.dot_general(a, b, NT, preferred_element_type=F32)


def nn(a, b):
    return jnp.dot(a, b, preferred_element_type=F32)


def z_of(i, n_sub):
    return (i % 2) * (n_sub // 2) + i // 2


def kernel(
    n_sub, n_rng, sections, stages, cap,
    e_ref, chirp_ref, off_ref, own_ref, aim_ref, w_ref, out_ref,
    h_ref, tail, metas, wall, cmp, img, gt, ya, yb, pick, upper, labsend, lab, lrow, place, sbuf, got, tbuf, obuf,
    tail_s, tail_r, meta_s, meta_r, w_s, w_r, img_s, img_r, lab_s, lab_r, x_s, x_r, t_s, t_r, loc,
):
    z = lax.axis_index("sub")
    r = lax.axis_index("rng")
    p = e_ref.shape[1]
    rd_len = e_ref.shape[2]
    taps_len = rd_len
    chunks = rd_len // CH
    width = CH + taps_len
    keep = stages > 1
    dests = n_sub * n_rng

    barrier = pltpu.get_barrier_semaphore()
    for d in range(1, n_sub):
        pl.semaphore_signal(barrier, inc=1, device_id=(lax.rem(z + d, n_sub), r), device_id_type=MESH)
    for d in range(1, n_rng):
        pl.semaphore_signal(barrier, inc=1, device_id=(z, lax.rem(r + d, n_rng)), device_id_type=MESH)

    taps = chirp_ref[...].astype(F32)
    parts = []
    for part in range(2):
        row = jnp.concatenate([taps[part : part + 1], jnp.zeros((1, CH), F32)], axis=1)
        parts.append(pltpu.roll(jnp.broadcast_to(row, (CH, width)), 0, 1, stride=1, stride_axis=0))
    h_re, h_im = parts
    h_ref[0, :CH] = h_re.astype(BF)
    h_ref[0, CH:] = (-h_im).astype(BF)
    h_ref[1, :CH] = h_im.astype(BF)
    h_ref[1, CH:] = h_re.astype(BF)

    for section in range(sections):
        for side in range(2):
            j = section * 2 + side
            off = off_ref[section, pl.ds(side, 1), :]
            both = []
            for part in range(2):
                w = w_ref[j * 2 + part].astype(F32)
                for bit in (1, 2, 4):
                    odd = jnp.broadcast_to((off // bit) % 2, (8, p)) == 1
                    w = jnp.where(odd, pltpu.roll(w, bit, 0), w)
                both.append(w)
            wall[z, j] = jnp.concatenate(both, axis=0).astype(BF)
            metas[z, pl.ds(j, 1), :] = off
    metas[z, pl.ds(6, 1), :] = own_ref[...]
    metas[z, pl.ds(7, 1), :] = aim_ref[...]
    for j in range(sections * 2, 6):
        metas[z, pl.ds(j, 1), :] = jnp.zeros((1, p), jnp.int32)
    pl.semaphore_wait(barrier, n_sub + n_rng - 2)

    def remote(src, dst, ss, rs, dev):
        return pltpu.make_async_remote_copy(
            src_ref=src, dst_ref=dst, send_sem=ss, recv_sem=rs, device_id=dev, device_id_type=MESH
        )

    def tail_copy(k):
        span = pl.ds(k * CH, CH)
        left = jnp.where(r == 0, 1, r - 1)
        return remote(e_ref.at[:, :, span], tail.at[:, :, span], tail_s.at[k], tail_r.at[k], (z, left))

    @pl.when(r > 0)
    def _():
        for k in range(chunks):
            tail_copy(k).start()

    def meta_copy(src, d):
        peer = lax.rem(z + d, n_sub)
        return (
            remote(metas.at[z], metas.at[src], meta_s.at[d], meta_r.at[src], (peer, r)),
            remote(wall.at[z], wall.at[src], w_s.at[d], w_r.at[src], (peer, r)),
        )

    for d in range(1, n_sub):
        for c in meta_copy(z, d):
            c.start()

    @pl.when(r == n_rng - 1)
    def _():
        tail[...] = jnp.zeros_like(tail)

    def build_merge(section, g, slot):
        for side in range(2):
            j = section * 2 + side
            off = metas[g, pl.ds(j, 1), :]
            w = wall[g, j].astype(F32)
            spot = lax.broadcasted_iota(jnp.int32, (p, p), 0) - off
            hit = (spot >= 0) & (spot < 8)
            for part in range(2):
                wide = jnp.broadcast_to(w[part * 8 : part * 8 + 8][None], (p // 8, 8, p)).reshape(p, p)
                gt[slot, side * p : side * p + p, part * p : part * p + p] = jnp.where(hit, wide, 0.0).astype(BF)

    def build_pick(g, slot):
        owner = metas[g, pl.ds(6, 1), :]
        aim = metas[g, pl.ds(7, 1), :]
        onehot = jnp.where(lax.broadcasted_iota(jnp.int32, (dests, p), 0) == owner, 1.0, 0.0)
        before = nn(onehot.astype(BF), upper[...])
        rank = jnp.sum(onehot * before, axis=0, keepdims=True).astype(jnp.int32)
        zd = owner // n_rng
        where_to = ((owner - zd * n_rng) * n_sub + zd) * cap + rank
        hit = lax.broadcasted_iota(jnp.int32, (dests * cap, p), 0) == where_to
        pick[slot] = jnp.where(hit, 1.0, 0.0).astype(BF)
        mark = aim + 1
        hi = mark // 16
        lo = mark - hi * 16
        rows = lax.broadcasted_iota(jnp.int32, (16, p), 0)
        both = jnp.where(rows == 0, hi, jnp.where(rows == 1, lo, 0)).astype(F32).astype(BF)
        out = nt(both, pick[slot])
        label = out[0:1] * 16.0 + out[1:2] - 1.0
        for rd in range(n_rng):
            labsend[rd, pl.ds(g, 1), :] = label[:, rd * 128 : (rd + 1) * 128]

    before = lax.broadcasted_iota(jnp.int32, (p, p), 0) < lax.broadcasted_iota(jnp.int32, (p, p), 1)
    upper[...] = jnp.where(before, 1.0, 0.0).astype(BF)

    def img_copy(s, i, src):
        sub = s * n_sub + i
        k, o = sub // (CH // CS), sub % (CH // CS)
        view = cmp.at[k, :, pl.ds(o * CS, CS), :]
        zd = z_of(i, n_sub)
        return view, remote(view, img.at[s, src], img_s.at[s, i], img_r.at[s, src], (zd, r))

    def wait_meta(g):
        @pl.when(z != g)
        def _():
            for c in meta_copy(g, 1):
                c.wait_recv()

    for k in range(chunks):
        @pl.when(r < n_rng - 1)
        def _():
            tail_copy(k).wait_recv()

        cut = rd_len - CH * k
        acc = None
        for part in range(2):
            x = nt(h_ref[part, :, :cut], e_ref[part, :, CH * k :])
            y = nt(h_ref[part, :, cut:], tail[part, :, : CH * (k + 1)])
            acc = x + y if acc is None else acc + x + y
        cmp[k] = acc.astype(BF).reshape(2, CH, p)
        for o in range(CH // CS):
            sub = k * (CH // CS) + o
            s, i = sub // n_sub, sub % n_sub
            view, copy = img_copy(s, i, z)
            own = z == z_of(i, n_sub)

            @pl.when(own)
            def _():
                pltpu.make_async_copy(view, img.at[s, z], loc.at[s]).start()

            @pl.when(jnp.logical_not(own))
            def _():
                copy.start()

        if keep and k < n_sub:
            wait_meta(k)
            build_merge(0, k, k)

    for g in range(n_sub):
        if not keep or g >= chunks:
            wait_meta(g)
        if keep:
            for section in range(1 if g < chunks else 0, sections):
                build_merge(section, g, section * n_sub + g)
            build_pick(g, g)

    def lab_copy(src, d):
        peer = lax.rem(r + d, n_rng)
        return remote(labsend.at[peer], lab.at[src], lab_s.at[d], lab_r.at[src], (z, peer))

    def send_labels():
        for d in range(1, n_rng):
            lab_copy(r, d).start()
        lab[r] = labsend[r]

    def x_copy(s, src, d):
        peer = lax.rem(r + d, n_rng)
        return remote(sbuf.at[s, peer], got.at[s, :, src], x_s.at[s, d], x_r.at[s, src], (z, peer))

    def x_local(s):
        return pltpu.make_async_copy(sbuf.at[s, r], got.at[s, :, r], loc.at[stages + s])

    if keep:
        send_labels()

    for s in range(stages):
        pltpu.make_async_copy(img.at[s, z], img.at[s, z], loc.at[s]).wait()
        for section in range(sections):
            bit = 1 << section
            dst = (ya, yb)[section % 2]

            def load(g):
                if section == 0:
                    return img[s, g].reshape(2 * CS, p)
                return (ya, yb)[(section + 1) % 2][g]

            def merge(g, carry):
                q = g + bit - 2 * bit * ((g // bit) % 2)
                slot = section * n_sub + g
                if not keep:
                    slot = 0
                    build_merge(section, g, 0)
                both = nn(jnp.concatenate([load(g), load(q)], axis=1), gt[slot])
                a, b = both[:, :p], both[:, p:]
                dst[g, :CS] = (a[:CS] - b[CS:]).astype(BF)
                dst[g, CS:] = (a[CS:] + b[:CS]).astype(BF)
                return carry

            if section == 0:
                for away in range(n_sub // 2):
                    pair = lax.rem(z // 2 + away, n_sub // 2)
                    if away == 0:
                        img_copy(s, 0, z + 1 - 2 * (z % 2))[1].wait_recv()
                    else:
                        img_copy(s, 0, 2 * pair)[1].wait_recv()
                        img_copy(s, 0, 2 * pair + 1)[1].wait_recv()
                    lax.fori_loop(2 * pair, 2 * pair + 2, merge, 0)
            else:
                lax.fori_loop(0, n_sub, merge, 0)
        final = (ya, yb)[(sections - 1) % 2]

        def gather(g, carry):
            slot = g
            if not keep:
                slot = 0
                build_pick(g, 0)
            rows = nt(pick[slot], final[g]).astype(BF)
            sbuf[s, :, :, pl.ds(pl.multiple_of(g * cap, cap), cap), :] = rows.reshape(n_rng, n_sub, cap, 2 * CS)
            return carry

        lax.fori_loop(0, n_sub, gather, 0)
        for d in range(1, n_rng):
            x_copy(s, r, d).start()
        x_local(s).start()
        if not keep:
            send_labels()

    for d in range(1, n_rng):
        lab_copy(lax.rem(r + d, n_rng), d).wait_recv()
    lane = lax.broadcasted_iota(jnp.int32, (n_rng, 128), 1) // cap
    for zd in range(n_sub):
        total = jnp.zeros((n_rng, 128), F32)
        for g in range(n_sub):
            piece = lab[:, g, :]
            move = ((g - zd) * cap) % 128
            if move:
                piece = pltpu.roll(piece, move, 1)
            total = jnp.where(lane == g, piece, total)
        lrow[zd] = total

    def build_place(zd, slot):
        rows = lax.broadcasted_iota(jnp.int32, (p, 128), 0)
        for j in range(n_rng):
            label = lrow[zd, pl.ds(j, 1), :].astype(jnp.int32)
            place[slot, :, j * 128 : (j + 1) * 128] = jnp.where(rows == label, 1.0, 0.0).astype(BF)

    if keep:
        def run(zd, carry):
            build_place(zd, zd)
            return carry

        lax.fori_loop(0, n_sub, run, 0)

    def flip(bits):
        at = z
        for j in range(bits.bit_length()):
            if bits >> j & 1:
                at = at + (1 << j) - (2 << j) * ((z // (1 << j)) % 2)
        return at

    def t_copy(s, src, zd, d):
        return remote(tbuf.at[s, zd], obuf.at[s, src], t_s.at[s, d], t_r.at[s, src], (zd, r))

    for s in range(stages):
        x_local(s).wait()
        for d in range(1, n_rng):
            x_copy(s, lax.rem(r + d, n_rng), d).wait_recv()
        for d in range(n_sub - 1, -1, -1):
            zd = flip(d)
            slot = zd
            if not keep:
                slot = 0
                build_place(zd, 0)
            tile = nn(place[slot], got[s, zd].reshape(n_rng * 128, 2 * CS)).astype(BF)
            if d:
                tbuf[s, zd] = tile
                t_copy(s, z, zd, d).start()
            else:
                obuf[s, z] = tile

    for s in range(stages):
        for d in range(1, n_sub):
            peer = lax.rem(z + d, n_sub)
            t_copy(s, peer, peer, d).wait_recv()
        for i in range(0, n_sub, 2):
            low, high = obuf[s, z_of(i, n_sub)], obuf[s, z_of(i + 1, n_sub)]
            span = slice((s * n_sub + i) * CS, (s * n_sub + i + 2) * CS)
            out_ref[0, :, span] = jnp.concatenate([low[:, :CS], high[:, :CS]], axis=1)
            out_ref[1, :, span] = jnp.concatenate([low[:, CS:], high[:, CS:]], axis=1)

    @pl.when(r > 0)
    def _():
        for k in range(chunks):
            tail_copy(k).wait_send()

    for d in range(1, n_sub):
        for c in meta_copy(z, d):
            c.wait_send()
    for s in range(stages):
        for i in range(n_sub):
            @pl.when(z != z_of(i, n_sub))
            def _():
                img_copy(s, i, z)[1].wait_send()

        for d in range(1, n_rng):
            x_copy(s, r, d).wait_send()
        for d in range(1, n_sub):
            t_copy(s, z, flip(d), d).wait_send()
    for d in range(1, n_rng):
        lab_copy(r, d).wait_send()


def on_device(echoes, chirp, offsets, weights, owners, targets):
    p = echoes.shape[1]
    r_dev = echoes.shape[2]
    n_sub = lax.axis_size("sub")
    n_rng = lax.axis_size("rng")
    devices = n_sub * n_rng
    sections = offsets.shape[0]
    cap = max(16, 2 * p // devices)
    stages = r_dev // (n_sub * CS)
    chunks = r_dev // CH
    keep = stages > 1
    vm = pltpu.VMEM
    dma = pltpu.SemaphoreType.DMA
    built = n_sub if keep else 1
    scratch = [
        vm((2, 2 * CH, CH + r_dev), BF),
        vm((2, p, r_dev), BF),
        vm((n_sub, 8, p), jnp.int32),
        vm((n_sub, sections * 2, 16, p), BF),
        vm((chunks, 2, CH, p), BF),
        vm((stages, n_sub, 2, CS, p), BF),
        vm((built * sections if keep else 1, 2 * p, 2 * p), BF),
        vm((n_sub, 2 * CS, p), BF),
        vm((n_sub, 2 * CS, p), BF),
        vm((built, devices * cap, p), BF),
        vm((p, p), BF),
        vm((n_rng, 8, 128), F32),
        vm((n_rng, 8, 128), F32),
        vm((n_sub, n_rng, 128), F32),
        vm((built, p, n_rng * 128), BF),
        vm((stages, n_rng, n_sub, n_sub * cap, 2 * CS), BF),
        vm((stages, n_sub, n_rng, n_sub * cap, 2 * CS), BF),
        vm((stages, n_sub, p, 2 * CS), BF),
        vm((stages, n_sub, p, 2 * CS), BF),
        dma((chunks,)), dma((chunks,)),
        dma((n_sub,)), dma((n_sub,)),
        dma((n_sub,)), dma((n_sub,)),
        dma((stages, n_sub)), dma((stages, n_sub)),
        dma((n_rng,)), dma((n_rng,)),
        dma((stages, n_rng)), dma((stages, n_rng)),
        dma((stages, n_sub)), dma((stages, n_sub)),
        dma((2 * stages,)),
    ]
    return pl.pallas_call(
        functools.partial(kernel, n_sub, n_rng, sections, stages, cap),
        out_shape=jax.ShapeDtypeStruct((2, p, r_dev), BF),
        in_specs=[pl.BlockSpec(memory_space=pltpu.VMEM)] * 6,
        out_specs=pl.BlockSpec(memory_space=pltpu.VMEM),
        scratch_shapes=scratch,
        compiler_params=pltpu.CompilerParams(
            collective_id=0, has_side_effects=True, vmem_limit_bytes=56 * 1024 * 1024
        ),
        cost_estimate=pl.CostEstimate(flops=8 * 10**9, bytes_accessed=4 * 10**6, transcendentals=0),
    )(
        echoes,
        chirp,
        offsets[:, 0],
        owners.reshape(1, p),
        targets.reshape(1, p),
        weights.transpose(0, 1, 2, 3, 5, 4).reshape(sections * 4, weights.shape[-1], p),
    )


def solution(mesh):
    in_specs = (
        P(None, "sub", "rng"),
        P(),
        P(None, "sub", None, None),
        P(None, "sub", None, None, None, None),
        P("sub", "rng", None, None),
        P("sub", "rng", None),
    )
    out_specs = P(None, "sub", "rng")
    return jax.shard_map(
        on_device, mesh=mesh, in_specs=in_specs, out_specs=out_specs, check_vma=False
    )
```
